32 devices in a mesh: slide: 2 (over x), row: 16 (over z, y, core).
Axes of the slice: x: 2, y: 2, z: 4, core: 2. Of those that a mesh axis runs over, the one named last changes fastest.
Arguments:
- tokens: bfloat16 [128, 128, 768], P(('slide', 'row')), parts along dimension 0, may hold values from -6 to 6
- norm_gain: float32 [768], replicated, may hold values from 0.1 to 1.9
- query_weight: bfloat16 [768, 768], replicated, may hold values from -0.875 to 0.875
- key_weight: bfloat16 [768, 768], replicated, may hold values from -0.875 to 0.875
- value_weight: bfloat16 [768, 768], replicated, may hold values from -0.21875 to 0.21875
- out_weight: bfloat16 [768, 768], replicated, may hold values from -0.21875 to 0.21875
- head_scale: float32 [12], replicated, may hold values from 0.02 to 0.5
- pool_queries: bfloat16 [16, 768], replicated, may hold values from -24 to 24
Outputs:
- mixed: bfloat16 [128, 128, 768], P(('slide', 'row')), parts along dimension 0
- pooled: float32 [32, 768], P('slide'), parts along dimension 0
The draws below stay inside these ranges and needn't reach their ends.
There are 2 independent parts, one for each index of `slide`. The reference program is written for one: setup_inputs(seed, part) draws one part's arguments, and reference() takes and returns one part's arrays. A program takes and returns all parts, laid end to end along the dimension named above; an argument that names none is the same for every part. Nothing has to cross between parts.
All inputs are finite; a program needn't handle non-finite values.
Results may differ from the reference program's by a relative error of at most 0.007.
The reference program's roundings to bfloat16 on the way count: a program that leaves them out, or rounds other values in their place, can miss the bound.
Values may be sent and summed in bfloat16 or wider, within the bound.
A program may use at most 128 MiB of HBM per device.

```python
import math
import jax
import jax.numpy as jnp
from jax import lax

HEADS = 12
D = 768
RAD = 4
PQ = 16
ROWS_DEV = 4
COLS = 128
SLAB_ROWS = 64


def block_levels(stream_key, dims, shards, low, high):
    gain, own = 1.0, jax.random.fold_in(stream_key, 6)
    for position, parts in shards:
        heights = jnp.exp(jax.random.uniform(jax.random.fold_in(own, position), (parts,), jnp.float32, low / len(shards), high / len(shards)))
        gain = gain * jnp.repeat(heights, dims[position] // parts).reshape([-1 if axis == position else 1 for axis in range(len(dims))])
    return gain


def centred(rng, shape, scale, limit, shards=(), held_as=jnp.bfloat16):
    result = scale * jax.random.normal(rng, shape, jnp.float32)
    if shards:
        result = result * block_levels(rng, shape, shards, -0.22, 0.18)
    return jnp.clip(result, -limit, limit).astype(held_as)


def setup_inputs(seed: int = 0, part: int = 0) -> dict:
    key_of = jax.random.split(jax.random.key(seed), 9)
    part_keys = jax.random.split(jax.random.fold_in(key_of[8], part), 9)
    return {
        "tokens": centred(part_keys[0], (SLAB_ROWS, COLS, D), 1.0, 6.0, ((0, 16),)),
        "norm_gain": jnp.clip(1.0 + 0.18 * jax.random.normal(key_of[1], (D,), jnp.float32), 0.1, 1.9),
        "query_weight": centred(key_of[2], (D, D), (D // 16) ** -0.5, 0.875),
        "key_weight": centred(key_of[3], (D, D), (D // 16) ** -0.5, 0.875),
        "value_weight": centred(key_of[4], (D, D), D ** -0.5, 0.21875),
        "out_weight": centred(key_of[5], (D, D), D ** -0.5, 0.21875),
        "head_scale": jnp.clip(jnp.exp(jax.random.uniform(key_of[6], (HEADS,), jnp.float32, math.log(0.02), math.log(0.5))), 0.02, 0.5),
        "pool_queries": centred(key_of[7], (PQ, D), 4.0, 24.0),
    }


norm_eps = 1e-06

def normalize(tokens, norm_gain):
    feats = tokens.astype(jnp.float32)
    mean_sq = lax.optimization_barrier(jnp.mean(feats * feats, axis=-1, keepdims=True))
    return (feats * lax.rsqrt(mean_sq + norm_eps) * norm_gain).astype(jnp.bfloat16)

def project(weight, normed, head_count):
    row_count, col_count, feature_width = normed.shape
    flattened = normed.reshape(row_count * col_count, feature_width)
    projected = lax.dot_general(weight, flattened, (((0,), (1,)), ((), ())), preferred_element_type=jnp.float32)
    return projected.astype(jnp.bfloat16).reshape(head_count, feature_width // head_count, row_count, col_count)

def lorentz_time(spatial):
    spatial_f = spatial.astype(jnp.float32)
    return jnp.sqrt(1.0 + lax.optimization_barrier(jnp.sum(spatial_f * spatial_f, axis=1)))

def split_cols(array, group, block, reach):
    blocks = group // block
    lead = array.shape[:-1]
    main_part = array[..., :group].reshape(lead + (blocks, block))
    extra = array[..., block:]
    pad_width = [(0, 0)] * len(lead) + [(0, blocks * block - extra.shape[-1])]
    extra = jnp.pad(extra, pad_width).reshape(lead + (blocks, block))[..., :2 * reach]
    return jnp.concatenate([main_part, extra], axis=-1)

def window_attend(query_heads, key_rows, value_rows, row_inside, head_scale):
    head_count, head_width, row_count, col_count = query_heads.shape
    group = 128 if col_count % 128 == 0 else col_count
    block = 32 if group % 32 == 0 else 16
    blocks = group // block
    tile_rows = 4
    key_tile_rows = tile_rows + 2 * RAD
    key_tile_cols = block + 2 * RAD
    key_pad = jnp.pad(key_rows, ((0, 0), (0, 0), (0, 0), (RAD, RAD)))
    value_pad = jnp.pad(value_rows, ((0, 0), (0, 0), (0, 0), (RAD, RAD)))
    key_time = lorentz_time(key_pad)
    value_time = lorentz_time(value_pad)
    query_time = lorentz_time(query_heads)
    col_global = jnp.arange(col_count + 2 * RAD, dtype=jnp.int32) - RAD
    col_inside = (col_global >= 0) & (col_global < col_count)
    query_row = jnp.arange(tile_rows, dtype=jnp.int32)[:, None, None, None]
    query_col = jnp.arange(block, dtype=jnp.int32)[None, :, None, None]
    key_row = jnp.arange(key_tile_rows, dtype=jnp.int32)[None, None, :, None]
    key_col = jnp.arange(key_tile_cols, dtype=jnp.int32)[None, None, None, :]
    row_gap = key_row - query_row
    col_gap = key_col - query_col
    window_mask = (row_gap >= 0) & (row_gap <= 2 * RAD) & (col_gap >= 0) & (col_gap <= 2 * RAD)
    window_mask = window_mask.reshape(tile_rows * block, key_tile_rows * key_tile_cols)
    col_groups = col_count // group
    tile_count = row_count // tile_rows * col_groups

    def one_tile(tile_index):
        row_start = (tile_index // col_groups * tile_rows).astype(jnp.int32)
        col_start = (tile_index % col_groups * group).astype(jnp.int32)
        zero = jnp.zeros((), jnp.int32)
        query_tile = lax.dynamic_slice(query_heads, (zero, zero, row_start, col_start), (head_count, head_width, tile_rows, group))
        key_tile = lax.dynamic_slice(key_pad, (zero, zero, row_start, col_start), (head_count, head_width, key_tile_rows, group + 2 * RAD))
        value_tile = lax.dynamic_slice(value_pad, (zero, zero, row_start, col_start), (head_count, head_width, key_tile_rows, group + 2 * RAD))
        qtime_tile = lax.dynamic_slice(query_time, (zero, row_start, col_start), (head_count, tile_rows, group))
        ktime_tile = lax.dynamic_slice(key_time, (zero, row_start, col_start), (head_count, key_tile_rows, group + 2 * RAD))
        vtime_tile = lax.dynamic_slice(value_time, (zero, row_start, col_start), (head_count, key_tile_rows, group + 2 * RAD))
        rin_tile = lax.dynamic_slice_in_dim(row_inside, row_start, key_tile_rows, 0)
        cin_tile = lax.dynamic_slice_in_dim(col_inside, col_start, group + 2 * RAD, 0)
        query_blocks = query_tile.reshape(head_count, head_width, tile_rows, blocks, block)
        query_blocks = query_blocks.transpose(0, 3, 1, 2, 4).reshape(head_count, blocks, head_width, tile_rows * block)
        key_blocks = split_cols(key_tile, group, block, RAD).transpose(0, 3, 1, 2, 4)
        key_blocks = key_blocks.reshape(head_count, blocks, head_width, key_tile_rows * key_tile_cols)
        value_blocks = split_cols(value_tile, group, block, RAD).transpose(0, 3, 1, 2, 4)
        value_blocks = value_blocks.reshape(head_count, blocks, head_width, key_tile_rows * key_tile_cols)
        qtime_blocks = qtime_tile.reshape(head_count, tile_rows, blocks, block).transpose(0, 2, 1, 3)
        qtime_blocks = qtime_blocks.reshape(head_count, blocks, tile_rows * block)
        ktime_blocks = split_cols(ktime_tile, group, block, RAD).transpose(0, 2, 1, 3)
        ktime_blocks = ktime_blocks.reshape(head_count, blocks, key_tile_rows * key_tile_cols)
        vtime_blocks = split_cols(vtime_tile, group, block, RAD).transpose(0, 2, 1, 3)
        vtime_blocks = vtime_blocks.reshape(head_count, blocks, key_tile_rows * key_tile_cols)
        cin_blocks = split_cols(cin_tile, group, block, RAD)
        key_valid = rin_tile[:, None, None] & cin_blocks[None]
        key_valid = key_valid.transpose(1, 0, 2).reshape(blocks, key_tile_rows * key_tile_cols)
        inner = jnp.einsum('hbdq,hbdk->hbqk', query_blocks, key_blocks, preferred_element_type=jnp.float32)
        lorentz_dot = inner - qtime_blocks[:, :, :, None] * ktime_blocks[:, :, None, :]
        scores_now = head_scale[:, None, None, None] * (2.0 + 2.0 * lorentz_dot)
        allowed = window_mask[None, None] & key_valid[None, :, None, :]
        scores_now = jnp.where(allowed, scores_now, -jnp.inf)
        peak_score = lax.optimization_barrier(jnp.max(scores_now, axis=-1, keepdims=True))
        weights = jnp.exp(scores_now - peak_score).astype(jnp.bfloat16)
        mean_space = jnp.einsum('hbqk,hbdk->hbdq', weights, value_blocks, preferred_element_type=jnp.float32)
        mean_time = lax.optimization_barrier(jnp.sum(weights.astype(jnp.float32) * vtime_blocks[:, :, None, :], axis=-1))
        spread = jnp.sqrt(mean_time * mean_time - lax.optimization_barrier(jnp.sum(mean_space * mean_space, axis=2)))
        attended = (mean_space / spread[:, :, None, :]).astype(jnp.bfloat16)
        attended = attended.reshape(head_count, blocks, head_width, tile_rows, block).transpose(0, 2, 3, 1, 4)
        return attended.reshape(head_count, head_width, tile_rows, group)
    tiles = lax.map(one_tile, jnp.arange(tile_count, dtype=jnp.int32))
    tiles = tiles.reshape(row_count // tile_rows, col_groups, head_count, head_width, tile_rows, group)
    return tiles.transpose(2, 3, 0, 4, 1, 5).reshape(head_count, head_width, row_count, col_count)

def mix_out(attended, out_weight, token_block):
    head_count, head_width, row_count, col_count = attended.shape
    flattened = attended.reshape(head_count * head_width, row_count * col_count)
    projected = lax.dot_general(flattened, out_weight, (((0,), (0,)), ((), ())), preferred_element_type=jnp.float32)
    projected = projected.reshape(row_count, col_count, head_count * head_width)
    return (token_block.astype(jnp.float32) + projected).astype(jnp.bfloat16)

def pool_scores(pool_queries, key_heads, head_scale):
    head_count, head_width = (key_heads.shape[0], key_heads.shape[1])
    key_flat = key_heads.reshape(head_count, head_width, -1)
    pool_space = pool_queries.astype(jnp.float32).reshape(pool_queries.shape[0], head_count, head_width)
    pool_time = jnp.sqrt(1.0 + lax.optimization_barrier(jnp.sum(pool_space * pool_space, axis=-1)))
    lorentz_dot = jnp.einsum('phd,hdt->pht', pool_space, key_flat.astype(jnp.float32), precision=lax.Precision.HIGHEST)
    lorentz_dot = lorentz_dot - pool_time[:, :, None] * lorentz_time(key_flat)[None]
    return head_scale[None, :, None] * (2.0 + 2.0 * lorentz_dot)

def pool_partial(pool_score, peak_score, value_heads):
    head_count, head_width = (value_heads.shape[0], value_heads.shape[1])
    value_flat = value_heads.reshape(head_count, head_width, -1)
    weights = jnp.exp(pool_score - peak_score[:, :, None])
    mean_space = jnp.einsum('pht,hdt->phd', weights, value_flat.astype(jnp.float32), precision=lax.Precision.HIGHEST)
    mean_time = lax.optimization_barrier(jnp.sum(weights * lorentz_time(value_flat)[None], axis=-1))
    return (mean_space, mean_time)

def finish_pool(mean_space, mean_time):
    spread = jnp.sqrt(mean_time * mean_time - lax.optimization_barrier(jnp.sum(mean_space * mean_space, axis=-1)))
    pooled = mean_space / spread[:, :, None]
    return pooled.reshape(pooled.shape[0], -1)

def reference(tokens, norm_gain, query_weight, key_weight, value_weight, out_weight, head_scale, pool_queries):
    normed = normalize(tokens, norm_gain)
    query_heads = project(query_weight, normed, HEADS)
    key_heads = project(key_weight, normed, HEADS)
    value_heads = project(value_weight, normed, HEADS)
    key_rows = jnp.pad(key_heads, ((0, 0), (0, 0), (RAD, RAD), (0, 0)))
    value_rows = jnp.pad(value_heads, ((0, 0), (0, 0), (RAD, RAD), (0, 0)))

    def one_block(block_index):
        row_start = (block_index * ROWS_DEV).astype(jnp.int32)
        query_block = lax.dynamic_slice_in_dim(query_heads, row_start, ROWS_DEV, 2)
        key_block = lax.dynamic_slice_in_dim(key_rows, row_start, ROWS_DEV + 2 * RAD, 2)
        value_block = lax.dynamic_slice_in_dim(value_rows, row_start, ROWS_DEV + 2 * RAD, 2)
        token_block = lax.dynamic_slice_in_dim(tokens, row_start, ROWS_DEV, 0)
        global_rows = row_start - RAD + jnp.arange(ROWS_DEV + 2 * RAD, dtype=jnp.int32)
        row_inside = (global_rows >= 0) & (global_rows < SLAB_ROWS)
        attended = window_attend(query_block, key_block, value_block, row_inside, head_scale)
        return mix_out(attended, out_weight, token_block)
    block_count = SLAB_ROWS // ROWS_DEV
    mixed = lax.map(one_block, jnp.arange(block_count, dtype=jnp.int32))
    mixed = mixed.reshape(SLAB_ROWS, COLS, D)
    pool_score = pool_scores(pool_queries, key_heads, head_scale)
    peak_score = lax.optimization_barrier(jnp.max(pool_score, axis=-1))
    mean_space, mean_time = pool_partial(pool_score, peak_score, value_heads)
    pooled = finish_pool(mean_space, mean_time)
    return (mixed, pooled)
```

```python
import functools
import math

import jax
import jax.numpy as jnp
import numpy as np
from jax import lax
from jax.experimental import pallas as pl
from jax.experimental.pallas import tpu as pltpu
from jax.sharding import PartitionSpec as P

RAD = 4
EPS = 1e-06
PAD = 8
BLOCK = 32
WIN = BLOCK + 2 * PAD
RING = 48
LOG2E = math.log2(math.e)
FAR = -(2.0**30)
MESH = pl.DeviceIdType.MESH
BF = jnp.bfloat16
F32 = jnp.float32
NT = (((1,), (1,)), ((), ()))


def tables(heads, width, rows, cols):
    hw = width // heads
    t6, t3 = 6 * heads, 3 * heads
    row0, col0 = t6, t6 + rows
    pool_lane = col0 + RING
    assert pool_lane < 128
    lane = np.arange(128)
    head_of = np.arange(width) // hw
    ek = ((lane[None] // 6 == head_of[:, None]) & (lane[None] < t6)).astype(np.float32)
    ev = ((lane[None] // 3 == head_of[:, None]) & (lane[None] < t3)).astype(np.float32)
    sel = np.full((8, 128), 3.0, np.float32)
    sel[0, :t6] = np.tile([0, 1, 0, 1, 2, 0], heads)
    sel[1, :t6] = np.tile([0, 0, 1, 1, 0, 2], heads)
    sel[2, :t3] = np.tile([0, 1, 2], heads)
    pc = np.arange(cols + 2 * PAD) - PAD
    inside = (pc >= 0) & (pc < cols)
    kcol = np.zeros((cols + 2 * PAD, 128), np.float32)
    m = np.arange(RING)
    near = ((pc[:, None] - m[None] + RAD) % RING <= 2 * RAD) & inside[:, None]
    kcol[:, col0 : col0 + RING] = np.where(near, 0.0, FAR)
    kcol[:, pool_lane] = np.where(inside, 0.0, FAR)
    qcol = np.zeros((cols, 128), np.float32)
    qcol[np.arange(cols), col0 + np.arange(cols) % RING] = 1.0
    return (
        jnp.asarray(ek, BF), jnp.asarray(ev, BF), jnp.asarray(sel),
        jnp.asarray(kcol), jnp.asarray(qcol), row0, pool_lane,
    )


def kernel(
    n, heads, row0, pool_lane,
    tok_hbm, wq_hbm, wk_hbm, wv_hbm, wo_hbm, gain_ref, scale_ref, pq_ref,
    ek_ref, ev_ref, sel_ref, kcol_ref, qcol_ref,
    mixed_ref, pooled_ref,
    tok, wq, wk, wv, wo, halo, nrm, nrmq, kk, vv, qq, kaug, vaug, qaug, att, st, rc,
    load_sem, tok_send, tok_recv, st_send, st_recv,
):
    rows, cols, width = tok.shape
    pcols = cols + 2 * PAD
    steps = n.bit_length() - 1
    pairs = width // 128
    hw = width // heads
    blocks = cols // BLOCK
    krows = rows + 2 * RAD
    npq = pq_ref.shape[0]
    nt = 256 if width % 256 == 0 else 128
    me = lax.axis_index("row")

    loads = [
        pltpu.make_async_copy(src, dst, load_sem.at[i])
        for i, (src, dst) in enumerate(
            [(tok_hbm, tok), (wq_hbm, wq), (wk_hbm, wk), (wv_hbm, wv), (wo_hbm, wo)]
        )
    ]
    for load in loads:
        load.start()

    partners = [me + (1 - 2 * ((me // (1 << k)) % 2)) * (1 << k) for k in range(steps)]
    barrier = pltpu.get_barrier_semaphore()

    def signal(to):
        pl.semaphore_signal(barrier, inc=1, device_id={"row": to}, device_id_type=MESH)

    beside = lax.rem(me + n - 1 + 2 * (me % 2), n)
    for other in partners + [beside]:
        signal(other)
    pl.semaphore_wait(barrier, steps + 1)

    to_left = pltpu.make_async_remote_copy(
        tok_hbm.at[pl.ds(0, RAD)], halo.at[1], tok_send.at[0], tok_recv.at[1],
        device_id={"row": jnp.maximum(me - 1, 0)}, device_id_type=MESH)
    to_right = pltpu.make_async_remote_copy(
        tok_hbm.at[pl.ds(rows - RAD, RAD)], halo.at[0], tok_send.at[1], tok_recv.at[0],
        device_id={"row": jnp.minimum(me + 1, n - 1)}, device_id_type=MESH)
    pl.when(me > 0)(lambda: to_left.start())
    pl.when(me < n - 1)(lambda: to_right.start())

    lane = lax.broadcasted_iota(jnp.int32, (1, 128), 1)
    gain = gain_ref[...]

    def normalized(x):
        x = x.astype(F32)
        return x * lax.rsqrt(jnp.mean(x * x, axis=-1, keepdims=True) + EPS) * gain

    def padded(y):
        zero = jnp.zeros((PAD, y.shape[1]), F32)
        return jnp.concatenate([zero, y, zero], axis=0).astype(BF)

    def split(t, kind):
        hi = t.astype(BF).astype(F32)
        mid = (t - hi).astype(BF).astype(F32)
        low = t - hi - mid
        kind = sel_ref[kind : kind + 1, :]
        return jnp.where(kind == 0, hi, jnp.where(kind == 1, mid, jnp.where(kind == 2, low, 0.0)))

    def times(u, pick):
        u = u.astype(F32)
        sq = u * u
        hi = sq.astype(BF)
        low = (sq - hi.astype(F32)).astype(BF)
        total = jnp.dot(hi, pick, preferred_element_type=F32)
        total = total + jnp.dot(low, pick, preferred_element_type=F32)
        return jnp.sqrt(1.0 + total)

    def keys_values(first, count):
        flat = nrm[pl.ds(first, count)].reshape(count * pcols, width)

        def tile(j, _):
            part = pl.ds(pl.multiple_of(j * nt, nt), nt)
            k = jnp.dot(flat, wk[:, part], preferred_element_type=F32).astype(BF)
            kk[pl.ds(first, count), :, part] = k.reshape(count, pcols, nt)
            v = jnp.dot(flat, wv[:, part], preferred_element_type=F32).astype(BF)
            vv[pl.ds(first, count), :, part] = v.reshape(count, pcols, nt)
            return 0

        lax.fori_loop(0, width // nt, tile, 0)

        def aug(i, _):
            slot = first + i
            inside = jnp.logical_and(
                jnp.logical_or(slot >= RAD, me > 0), jnp.logical_or(slot < RAD + rows, me < n - 1))
            qrow = lane - row0
            seen = (qrow <= slot) & (qrow >= slot - 2 * RAD) & inside
            row_mask = jnp.where((qrow >= 0) & (qrow < rows) & ~seen, FAR, 0.0)
            kaug[slot] = (split(times(kk[slot], ek_ref[...]), 0) + row_mask + kcol_ref[...]).astype(BF)
            vaug[slot] = split(times(vv[slot], ev_ref[...]), 2).astype(BF)
            return 0

        lax.fori_loop(0, count, aug, 0)

    loads[0].wait()

    def own_norm(r, _):
        y = normalized(tok[r])
        nrmq[r] = y.astype(BF)
        nrm[RAD + r] = padded(y)
        return 0

    lax.fori_loop(0, rows, own_norm, 0)
    for load in loads[1:4]:
        load.wait()
    keys_values(RAD, rows)

    def query_tile(j, _):
        part = pl.ds(pl.multiple_of(j * nt, nt), nt)
        q = jnp.dot(nrmq[...].reshape(rows * cols, width), wq[:, part], preferred_element_type=F32)
        qq[:, :, part] = q.astype(BF).reshape(rows, cols, nt)
        return 0

    lax.fori_loop(0, width // nt, query_tile, 0)

    def query_aug(r, _):
        onehot = jnp.where(lane == row0 + r, 1.0, 0.0)
        qaug[r] = (qcol_ref[...] + onehot - split(times(qq[r], ek_ref[...]), 1)).astype(BF)
        return 0

    lax.fori_loop(0, rows, query_aug, 0)

    def head_pair(q, aug, p):
        zero = jnp.zeros((), BF)
        low = lane < hw
        out = []
        for i in range(2):
            h = 2 * p + i
            mine = low if i == 0 else ~low
            keep = ((lane >= 6 * h) & (lane < 6 * h + 6)) | (lane >= row0)
            out.append(jnp.concatenate(
                [jnp.where(mine, q, zero), jnp.where(keep, aug, zero)], axis=1))
        return jnp.concatenate(out, axis=0)

    pq_aug = (jnp.where(lane == pool_lane, 1.0, 0.0) - split(times(pq_ref[...], ek_ref[...]), 1)).astype(BF)

    own = pl.ds(RAD, rows)
    peaks = jnp.full((npq, 128), 0.0, F32)
    tsum = jnp.full((npq, 128), 1.0, F32)
    for p in range(pairs):
        part = pl.ds(128 * p, 128)
        keys = jnp.concatenate(
            [kk[own, :, part].reshape(rows * pcols, 128), kaug[own].reshape(rows * pcols, 128)], axis=1)
        vals = jnp.concatenate(
            [vv[own, :, part].reshape(rows * pcols, 128), vaug[own].reshape(rows * pcols, 128)], axis=1)
        d = lax.dot_general(head_pair(pq_ref[:, part], pq_aug, p), keys, NT, preferred_element_type=F32)
        top = jnp.max(d, axis=-1, keepdims=True)
        scaled = []
        for i in range(2):
            c = (2.0 * LOG2E) * scale_ref[2 * p + i]
            mine = slice(i * npq, (i + 1) * npq)
            scaled.append((d[mine] - top[mine]) * c)
            peaks = jnp.where(lane == 2 * p + i, top[mine] * c, peaks)
        f = jnp.exp2(jnp.concatenate(scaled, axis=0))
        hi = f.astype(BF)
        rest = f - hi.astype(F32)
        mid = rest.astype(BF)
        low = (rest - mid.astype(F32)).astype(BF)
        m = jnp.dot(jnp.concatenate([hi, mid, low], axis=0), vals, preferred_element_type=F32)
        m = m[: 2 * npq] + m[2 * npq : 4 * npq] + m[4 * npq :]
        st[0, :, part] = jnp.where(lane < hw, m[:npq, :128], m[npq:, :128])
        for i in range(2):
            h = 2 * p + i
            tv = jnp.where((lane >= 3 * h) & (lane < 3 * h + 3), m[i * npq : (i + 1) * npq, 128:], 0.0)
            tsum = jnp.where(lane == h, jnp.sum(tv, axis=-1, keepdims=True), tsum)
    st[0, :, width : width + 128] = peaks
    st[0, :, width + 128 : width + 256] = tsum

    swaps = [
        pltpu.make_async_remote_copy(
            st.at[k], rc.at[k], st_send.at[k], st_recv.at[k],
            device_id={"row": partners[k]}, device_id_type=MESH)
        for k in range(steps)
    ]
    swaps[0].start()

    def spread_heads(x, p):
        return jnp.where(lane < hw, x[:, 2 * p : 2 * p + 1], x[:, 2 * p + 1 : 2 * p + 2])

    def merge(k):
        swaps[k].wait()
        peak_mine, peak_other = st[k, :, width : width + 128], rc[k, :, width : width + 128]
        peak = jnp.maximum(peak_mine, peak_other)
        f_mine, f_other = jnp.exp2(peak_mine - peak), jnp.exp2(peak_other - peak)
        st[k + 1, :, width : width + 128] = peak
        tpart = pl.ds(width + 128, 128)
        st[k + 1, :, tpart] = st[k, :, tpart] * f_mine + rc[k, :, tpart] * f_other
        for p in range(pairs):
            part = pl.ds(128 * p, 128)
            a = st[k, :, part] * spread_heads(f_mine, p)
            b = rc[k, :, part] * spread_heads(f_other, p)
            st[k + 1, :, part] = a + b
        if k + 1 < steps:
            swaps[k + 1].start()

    def side(i, first, there):
        @pl.when(there)
        def _():
            (to_right if i == 0 else to_left).wait_recv()

        @pl.when(jnp.logical_not(there))
        def _():
            halo[i] = jnp.zeros(halo.shape[1:], BF)

        def norm(r, _):
            nrm[first + r] = padded(normalized(halo[i, r]))
            return 0

        lax.fori_loop(0, RAD, norm, 0)
        keys_values(first, RAD)

    side(0, 0, me > 0)
    side(1, RAD + rows, me < n - 1)

    def attend(p, _):
        part = pl.ds(pl.multiple_of(128 * p, 128), 128)
        c0 = (2.0 * LOG2E) * scale_ref[2 * p]
        c1 = (2.0 * LOG2E) * scale_ref[2 * p + 1]
        for b in range(blocks):
            qs, ks = pl.ds(b * BLOCK, BLOCK), pl.ds(b * BLOCK, WIN)
            nq, nk = rows * BLOCK, krows * WIN
            q = head_pair(qq[:, qs, part].reshape(nq, 128), qaug[:, qs, :].reshape(nq, 128), p)
            keys = jnp.concatenate(
                [kk[:, ks, part].reshape(nk, 128), kaug[:, ks, :].reshape(nk, 128)], axis=1)
            vals = jnp.concatenate(
                [vv[:, ks, part].reshape(nk, 128), vaug[:, ks, :].reshape(nk, 128)], axis=1)
            d = lax.dot_general(q, keys, NT, preferred_element_type=F32)
            d = d - jnp.max(d, axis=-1, keepdims=True)
            e = jnp.concatenate([jnp.exp2(d[:nq] * c0), jnp.exp2(d[nq:] * c1)], axis=0).astype(BF)
            m = jnp.dot(e, vals, preferred_element_type=F32)
            out = []
            for i in range(2):
                h = 2 * p + i
                sp, tv = m[i * nq : (i + 1) * nq, :128], m[i * nq : (i + 1) * nq, 128:]
                mine = (lane < hw) if i == 0 else (lane >= hw)
                mt = jnp.sum(jnp.where((lane >= 3 * h) & (lane < 3 * h + 3), tv, 0.0), axis=-1, keepdims=True)
                ss = jnp.sum(jnp.where(mine, sp * sp, 0.0), axis=-1, keepdims=True)
                out.append(sp * lax.rsqrt(mt * mt - ss))
            att[:, qs, part] = jnp.where(lane < hw, out[0], out[1]).astype(BF).reshape(rows, BLOCK, 128)
        for k in range(steps):
            pl.when(p == min(k, pairs - 1))(functools.partial(merge, k))
        return 0

    lax.fori_loop(0, pairs, attend, 0)

    last = st.at[steps]
    mt = last[:, width + 128 : width + 256]
    for p in range(pairs):
        part = pl.ds(128 * p, 128)
        sp = last[:, part]
        sq = sp * sp
        ss = jnp.where(
            lane < hw,
            jnp.sum(jnp.where(lane < hw, sq, 0.0), axis=-1, keepdims=True),
            jnp.sum(jnp.where(lane < hw, 0.0, sq), axis=-1, keepdims=True))
        t = spread_heads(mt, p)
        pooled_ref[:, part] = sp / jnp.sqrt(t * t - ss)

    loads[4].wait()

    def out_tile(j, _):
        part = pl.ds(pl.multiple_of(j * nt, nt), nt)
        y = jnp.dot(att[...].reshape(rows * cols, width), wo[:, part], preferred_element_type=F32)
        y = y + tok[:, :, part].reshape(rows * cols, nt).astype(F32)
        mixed_ref[:, :, part] = y.astype(BF).reshape(rows, cols, nt)
        return 0

    lax.fori_loop(0, width // nt, out_tile, 0)
    pl.when(me > 0)(lambda: to_left.wait_send())
    pl.when(me < n - 1)(lambda: to_right.wait_send())


def per_device(n, tokens, norm_gain, wq, wk, wv, wo, head_scale, pool_queries):
    rows, cols, width = tokens.shape
    heads = head_scale.shape[0]
    npq = pool_queries.shape[0]
    steps = n.bit_length() - 1
    assert n == 1 << steps and rows >= RAD and cols % BLOCK == 0 and 2 * width == 128 * heads
    ek, ev, sel, kcol, qcol, row0, pool_lane = tables(heads, width, rows, cols)
    krows, pcols = rows + 2 * RAD, cols + 2 * PAD
    vm = pl.BlockSpec(memory_space=pltpu.VMEM)
    hbm = pl.BlockSpec(memory_space=pl.ANY)
    V = pltpu.VMEM
    wshape = V((width, width), BF)
    return pl.pallas_call(
        functools.partial(kernel, n, heads, row0, pool_lane),
        out_shape=(
            jax.ShapeDtypeStruct(tokens.shape, BF),
            jax.ShapeDtypeStruct((npq, width), F32),
        ),
        in_specs=[hbm] * 5 + [vm, pl.BlockSpec(memory_space=pltpu.SMEM)] + [vm] * 6,
        out_specs=(vm, vm),
        scratch_shapes=[
            V(tokens.shape, BF), wshape, wshape, wshape, wshape,
            V((2, RAD, cols, width), BF),
            V((krows, pcols, width), BF),
            V(tokens.shape, BF),
            V((krows, pcols, width), BF),
            V((krows, pcols, width), BF),
            V(tokens.shape, BF),
            V((krows, pcols, 128), BF),
            V((krows, pcols, 128), BF),
            V((rows, cols, 128), BF),
            V(tokens.shape, BF),
            V((steps + 1, npq, width + 256), F32),
            V((steps, npq, width + 256), F32),
            pltpu.SemaphoreType.DMA((5,)),
            pltpu.SemaphoreType.DMA((2,)),
            pltpu.SemaphoreType.DMA((2,)),
            pltpu.SemaphoreType.DMA((steps,)),
            pltpu.SemaphoreType.DMA((steps,)),
        ],
        compiler_params=pltpu.CompilerParams(
            collective_id=0, has_side_effects=True, vmem_limit_bytes=48 * 1024 * 1024),
    )(tokens, wq, wk, wv, wo, norm_gain.reshape(1, width), head_scale, pool_queries, ek, ev, sel, kcol, qcol)


def solution(mesh):
    placed = (P(("slide", "row"), None, None), P(), P(), P(), P(), P(), P(), P())
    return jax.shard_map(
        functools.partial(per_device, mesh.shape["row"]),
        mesh=mesh,
        in_specs=placed,
        out_specs=(P(("slide", "row"), None, None), P("slide", None)),
        check_vma=False,
    )
```

```python
import functools
import math

import jax
import jax.numpy as jnp
import numpy as np
from jax import lax
from jax.experimental import pallas as pl
from jax.experimental.pallas import tpu as pltpu
from jax.sharding import PartitionSpec as P

RAD = 4
EPS = 1e-06
PAD = 8
BLOCK = 32
WIN = BLOCK + 2 * PAD
RING = 48
LOG2E = math.log2(math.e)
FAR = -(2.0**30)
MESH = pl.DeviceIdType.MESH
BF = jnp.bfloat16
F32 = jnp.float32
NT = (((1,), (1,)), ((), ()))


def tables(heads, width, rows, cols):
    hw = width // heads
    t6, t3 = 6 * heads, 3 * heads
    row0, col0 = t6, t6 + rows
    pool_lane = col0 + RING
    assert pool_lane < 128
    lane = np.arange(128)
    head_of = np.arange(width) // hw
    ek = ((lane[None] // 6 == head_of[:, None]) & (lane[None] < t6)).astype(np.float32)
    ev = ((lane[None] // 3 == head_of[:, None]) & (lane[None] < t3)).astype(np.float32)
    sel = np.full((8, 128), 3.0, np.float32)
    sel[0, :t6] = np.tile([0, 1, 0, 1, 2, 0], heads)
    sel[1, :t6] = np.tile([0, 0, 1, 1, 0, 2], heads)
    sel[2, :t3] = np.tile([0, 1, 2], heads)
    pc = np.arange(cols + 2 * PAD) - PAD
    inside = (pc >= 0) & (pc < cols)
    kcol = np.zeros((cols + 2 * PAD, 128), np.float32)
    m = np.arange(RING)
    near = ((pc[:, None] - m[None] + RAD) % RING <= 2 * RAD) & inside[:, None]
    kcol[:, col0 : col0 + RING] = np.where(near, 0.0, FAR)
    kcol[:, pool_lane] = np.where(inside, 0.0, FAR)
    qcol = np.zeros((cols, 128), np.float32)
    qcol[np.arange(cols), col0 + np.arange(cols) % RING] = 1.0
    return (
        jnp.asarray(np.stack([ek, ev]), BF), jnp.asarray(np.concatenate([sel, kcol, qcol])),
        row0, pool_lane,
    )


def kernel(
    n, heads, row0, pool_lane,
    tok_hbm, wq_hbm, wk_hbm, wv_hbm, wo_hbm, pick_hbm, table_hbm, pq_hbm, gain_ref, scale_ref,
    mixed_ref, pooled_ref,
    tok, wq, wk, wv, wo, picks, table, pq_ref, halo, nrm, nrmq, kk, vv, qq, kaug, vaug, qaug, att, st, rc,
    load_sem, tok_send, tok_recv, st_send, st_recv,
):
    rows, cols, width = tok.shape
    pcols = cols + 2 * PAD
    steps = n.bit_length() - 1
    pairs = width // 128
    hw = width // heads
    blocks = cols // BLOCK
    krows = rows + 2 * RAD
    npq = pq_ref.shape[0]
    ek_ref, ev_ref = picks.at[0], picks.at[1]
    sel_ref = table.at[pl.ds(0, 8)]
    kcol_ref = table.at[pl.ds(8, pcols)]
    qcol_ref = table.at[pl.ds(8 + pcols, cols)]
    nt = 256 if width % 256 == 0 else 128
    me = lax.axis_index("row")

    loads = [
        pltpu.make_async_copy(src, dst, load_sem.at[i])
        for i, (src, dst) in enumerate(
            [(tok_hbm, tok), (wk_hbm, wk), (wv_hbm, wv), (pick_hbm, picks), (table_hbm, table), (pq_hbm, pq_ref), (wq_hbm, wq), (wo_hbm, wo)]
        )
    ]
    for load in loads:
        load.start()

    partners = [me + (1 - 2 * ((me // (1 << k)) % 2)) * (1 << k) for k in range(steps)]
    barrier = pltpu.get_barrier_semaphore()

    def signal(to):
        pl.semaphore_signal(barrier, inc=1, device_id={"row": to}, device_id_type=MESH)

    beside = lax.rem(me + n - 1 + 2 * (me % 2), n)
    for other in partners + [beside]:
        signal(other)
    pl.semaphore_wait(barrier, steps + 1)

    to_left = pltpu.make_async_remote_copy(
        tok_hbm.at[pl.ds(0, RAD)], halo.at[1], tok_send.at[0], tok_recv.at[1],
        device_id={"row": jnp.maximum(me - 1, 0)}, device_id_type=MESH)
    to_right = pltpu.make_async_remote_copy(
        tok_hbm.at[pl.ds(rows - RAD, RAD)], halo.at[0], tok_send.at[1], tok_recv.at[0],
        device_id={"row": jnp.minimum(me + 1, n - 1)}, device_id_type=MESH)
    even = me % 2 == 0
    pl.when(jnp.logical_and(even, me > 0))(lambda: to_left.start())
    pl.when(me < n - 1)(lambda: to_right.start())
    pl.when(jnp.logical_not(even))(lambda: to_left.start())

    lane = lax.broadcasted_iota(jnp.int32, (1, 128), 1)
    gain = gain_ref[...].reshape(1, width)

    def normalized(x):
        x = x.astype(F32)
        return x * lax.rsqrt(jnp.mean(x * x, axis=-1, keepdims=True) + EPS) * gain

    def padded(y):
        zero = jnp.zeros((PAD, y.shape[1]), F32)
        return jnp.concatenate([zero, y, zero], axis=0).astype(BF)

    def split(t, kind):
        hi = t.astype(BF).astype(F32)
        mid = (t - hi).astype(BF).astype(F32)
        low = t - hi - mid
        kind = sel_ref[kind : kind + 1, :]
        return jnp.where(kind == 0, hi, jnp.where(kind == 1, mid, jnp.where(kind == 2, low, 0.0)))

    def times(u, pick):
        u = u.astype(F32)
        sq = u * u
        hi = sq.astype(BF)
        low = (sq - hi.astype(F32)).astype(BF)
        total = jnp.dot(hi, pick, preferred_element_type=F32)
        total = total + jnp.dot(low, pick, preferred_element_type=F32)
        return jnp.sqrt(1.0 + total)

    def keys_values(first, count):
        flat = nrm[pl.ds(first, count)].reshape(count * pcols, width)

        def tile(j, _):
            part = pl.ds(pl.multiple_of(j * nt, nt), nt)
            k = jnp.dot(flat, wk[:, part], preferred_element_type=F32).astype(BF)
            kk[pl.ds(first, count), :, part] = k.reshape(count, pcols, nt)
            v = jnp.dot(flat, wv[:, part], preferred_element_type=F32).astype(BF)
            vv[pl.ds(first, count), :, part] = v.reshape(count, pcols, nt)
            return 0

        lax.fori_loop(0, width // nt, tile, 0)

        def aug(i, _):
            slot = first + i
            inside = jnp.logical_and(
                jnp.logical_or(slot >= RAD, me > 0), jnp.logical_or(slot < RAD + rows, me < n - 1))
            qrow = lane - row0
            seen = (qrow <= slot) & (qrow >= slot - 2 * RAD) & inside
            row_mask = jnp.where((qrow >= 0) & (qrow < rows) & ~seen, FAR, 0.0)
            kaug[slot] = (split(times(kk[slot], ek_ref[...]), 0) + row_mask + kcol_ref[...]).astype(BF)
            vaug[slot] = split(times(vv[slot], ev_ref[...]), 2).astype(BF)
            return 0

        lax.fori_loop(0, count, aug, 0)

    loads[0].wait()

    def own_norm(r, _):
        y = normalized(tok[r])
        nrmq[r] = y.astype(BF)
        nrm[RAD + r] = padded(y)
        return 0

    lax.fori_loop(0, rows, own_norm, 0)
    for load in loads[1:6]:
        load.wait()
    keys_values(RAD, rows)

    def head_pair(q, aug, p):
        zero = jnp.zeros((), BF)
        low = lane < hw
        out = []
        for i in range(2):
            h = 2 * p + i
            mine = low if i == 0 else ~low
            keep = ((lane >= 6 * h) & (lane < 6 * h + 6)) | (lane >= row0)
            out.append(jnp.concatenate(
                [jnp.where(mine, q, zero), jnp.where(keep, aug, zero)], axis=1))
        return jnp.concatenate(out, axis=0)

    pq_aug = (jnp.where(lane == pool_lane, 1.0, 0.0) - split(times(pq_ref[...], ek_ref[...]), 1)).astype(BF)

    own = pl.ds(RAD, rows)
    peaks = jnp.full((npq, 128), 0.0, F32)
    tsum = jnp.full((npq, 128), 1.0, F32)
    for p in range(pairs):
        part = pl.ds(128 * p, 128)
        keys = jnp.concatenate(
            [kk[own, :, part].reshape(rows * pcols, 128), kaug[own].reshape(rows * pcols, 128)], axis=1)
        vals = jnp.concatenate(
            [vv[own, :, part].reshape(rows * pcols, 128), vaug[own].reshape(rows * pcols, 128)], axis=1)
        d = lax.dot_general(head_pair(pq_ref[:, part], pq_aug, p), keys, NT, preferred_element_type=F32)
        top = jnp.max(d, axis=-1, keepdims=True)
        scaled = []
        for i in range(2):
            c = (2.0 * LOG2E) * scale_ref[2 * p + i]
            mine = slice(i * npq, (i + 1) * npq)
            scaled.append((d[mine] - top[mine]) * c)
            peaks = jnp.where(lane == 2 * p + i, top[mine] * c, peaks)
        f = jnp.exp2(jnp.concatenate(scaled, axis=0))
        hi = f.astype(BF)
        rest = f - hi.astype(F32)
        mid = rest.astype(BF)
        low = (rest - mid.astype(F32)).astype(BF)
        m = jnp.dot(jnp.concatenate([hi, mid, low], axis=0), vals, preferred_element_type=F32)
        m = m[: 2 * npq] + m[2 * npq : 4 * npq] + m[4 * npq :]
        st[0, :, part] = jnp.where(lane < hw, m[:npq, :128], m[npq:, :128])
        for i in range(2):
            h = 2 * p + i
            tv = jnp.where((lane >= 3 * h) & (lane < 3 * h + 3), m[i * npq : (i + 1) * npq, 128:], 0.0)
            tsum = jnp.where(lane == h, jnp.sum(tv, axis=-1, keepdims=True), tsum)
    st[0, :, width : width + 128] = peaks
    st[0, :, width + 128 : width + 256] = tsum

    swaps = [
        pltpu.make_async_remote_copy(
            st.at[k], rc.at[k], st_send.at[k], st_recv.at[k],
            device_id={"row": partners[k]}, device_id_type=MESH)
        for k in range(steps)
    ]
    swaps[0].start()

    def spread_heads(x, p):
        return jnp.where(lane < hw, x[:, 2 * p : 2 * p + 1], x[:, 2 * p + 1 : 2 * p + 2])

    def merge(k):
        swaps[k].wait()
        peak_mine, peak_other = st[k, :, width : width + 128], rc[k, :, width : width + 128]
        peak = jnp.maximum(peak_mine, peak_other)
        f_mine, f_other = jnp.exp2(peak_mine - peak), jnp.exp2(peak_other - peak)
        st[k + 1, :, width : width + 128] = peak
        tpart = pl.ds(width + 128, 128)
        st[k + 1, :, tpart] = st[k, :, tpart] * f_mine + rc[k, :, tpart] * f_other
        for p in range(pairs):
            part = pl.ds(128 * p, 128)
            a = st[k, :, part] * spread_heads(f_mine, p)
            b = rc[k, :, part] * spread_heads(f_other, p)
            st[k + 1, :, part] = a + b
        if k + 1 < steps:
            swaps[k + 1].start()

    loads[6].wait()

    def query_tile(j, _):
        part = pl.ds(pl.multiple_of(j * nt, nt), nt)
        q = jnp.dot(nrmq[...].reshape(rows * cols, width), wq[:, part], preferred_element_type=F32)
        qq[:, :, part] = q.astype(BF).reshape(rows, cols, nt)
        return 0

    lax.fori_loop(0, width // nt, query_tile, 0)

    def query_aug(r, _):
        onehot = jnp.where(lane == row0 + r, 1.0, 0.0)
        qaug[r] = (qcol_ref[...] + onehot - split(times(qq[r], ek_ref[...]), 1)).astype(BF)
        return 0

    lax.fori_loop(0, rows, query_aug, 0)

    merge(0)

    def arrived(i):
        pltpu.make_async_remote_copy(
            tok_hbm.at[pl.ds(0, RAD)], halo.at[i], tok_send.at[i], tok_recv.at[i],
            device_id={"row": beside}, device_id_type=MESH).wait_recv()

    def side_rows(i, first):
        def norm(r, _):
            nrm[first + r] = padded(normalized(halo[i, r]))
            return 0

        lax.fori_loop(0, RAD, norm, 0)
        keys_values(first, RAD)

    near, far = 1 - me % 2, me % 2
    inner = jnp.logical_and(me > 0, me < n - 1)
    arrived(near)
    side_rows(near, near * (RAD + rows))
    for k in range(1, min(steps, 3)):
        merge(k)

    @pl.when(inner)
    def _():
        arrived(far)

    @pl.when(jnp.logical_not(inner))
    def _():
        halo[far] = jnp.zeros(halo.shape[1:], BF)

    side_rows(far, far * (RAD + rows))

    def attend(p, _):
        part = pl.ds(pl.multiple_of(128 * p, 128), 128)
        c0 = (2.0 * LOG2E) * scale_ref[2 * p]
        c1 = (2.0 * LOG2E) * scale_ref[2 * p + 1]
        for b in range(blocks):
            qs, ks = pl.ds(b * BLOCK, BLOCK), pl.ds(b * BLOCK, WIN)
            nq, nk = rows * BLOCK, krows * WIN
            q = head_pair(qq[:, qs, part].reshape(nq, 128), qaug[:, qs, :].reshape(nq, 128), p)
            keys = jnp.concatenate(
                [kk[:, ks, part].reshape(nk, 128), kaug[:, ks, :].reshape(nk, 128)], axis=1)
            vals = jnp.concatenate(
                [vv[:, ks, part].reshape(nk, 128), vaug[:, ks, :].reshape(nk, 128)], axis=1)
            d = lax.dot_general(q, keys, NT, preferred_element_type=F32)
            d = d - jnp.max(d, axis=-1, keepdims=True)
            e = jnp.concatenate([jnp.exp2(d[:nq] * c0), jnp.exp2(d[nq:] * c1)], axis=0).astype(BF)
            m = jnp.dot(e, vals, preferred_element_type=F32)
            out = []
            for i in range(2):
                h = 2 * p + i
                sp, tv = m[i * nq : (i + 1) * nq, :128], m[i * nq : (i + 1) * nq, 128:]
                mine = (lane < hw) if i == 0 else (lane >= hw)
                mt = jnp.sum(jnp.where((lane >= 3 * h) & (lane < 3 * h + 3), tv, 0.0), axis=-1, keepdims=True)
                ss = jnp.sum(jnp.where(mine, sp * sp, 0.0), axis=-1, keepdims=True)
                out.append(sp * lax.rsqrt(mt * mt - ss))
            att[:, qs, part] = jnp.where(lane < hw, out[0], out[1]).astype(BF).reshape(rows, BLOCK, 128)
        for k in range(3, steps):
            pl.when(p == min(k - 3, pairs - 1))(functools.partial(merge, k))
        return 0

    lax.fori_loop(0, pairs, attend, 0)

    last = st.at[steps]
    mt = last[:, width + 128 : width + 256]
    for p in range(pairs):
        part = pl.ds(128 * p, 128)
        sp = last[:, part]
        sq = sp * sp
        ss = jnp.where(
            lane < hw,
            jnp.sum(jnp.where(lane < hw, sq, 0.0), axis=-1, keepdims=True),
            jnp.sum(jnp.where(lane < hw, 0.0, sq), axis=-1, keepdims=True))
        t = spread_heads(mt, p)
        pooled_ref[:, part] = sp / jnp.sqrt(t * t - ss)

    loads[7].wait()

    def out_tile(j, _):
        part = pl.ds(pl.multiple_of(j * nt, nt), nt)
        y = jnp.dot(att[...].reshape(rows * cols, width), wo[:, part], preferred_element_type=F32)
        y = y + tok[:, :, part].reshape(rows * cols, nt).astype(F32)
        mixed_ref[:, :, part] = y.astype(BF).reshape(rows, cols, nt)
        return 0

    lax.fori_loop(0, width // nt, out_tile, 0)
    pl.when(me > 0)(lambda: to_left.wait_send())
    pl.when(me < n - 1)(lambda: to_right.wait_send())


def per_device(n, tokens, norm_gain, wq, wk, wv, wo, head_scale, pool_queries):
    rows, cols, width = tokens.shape
    heads = head_scale.shape[0]
    npq = pool_queries.shape[0]
    steps = n.bit_length() - 1
    assert n == 1 << steps and rows >= RAD and cols % BLOCK == 0 and 2 * width == 128 * heads
    pick, table, row0, pool_lane = tables(heads, width, rows, cols)
    krows, pcols = rows + 2 * RAD, cols + 2 * PAD
    vm = pl.BlockSpec(memory_space=pltpu.VMEM)
    hbm = pl.BlockSpec(memory_space=pltpu.HBM)
    V = pltpu.VMEM
    wshape = V((width, width), BF)
    return pl.pallas_call(
        functools.partial(kernel, n, heads, row0, pool_lane),
        out_shape=(
            jax.ShapeDtypeStruct(tokens.shape, BF),
            jax.ShapeDtypeStruct((npq, width), F32),
        ),
        in_specs=[hbm] * 8 + [vm, pl.BlockSpec(memory_space=pltpu.SMEM)],
        out_specs=(vm, vm),
        scratch_shapes=[
            V(tokens.shape, BF), wshape, wshape, wshape, wshape,
            V(pick.shape, BF), V(table.shape, F32), V(pool_queries.shape, BF),
            V((2, RAD, cols, width), BF),
            V((krows, pcols, width), BF),
            V(tokens.shape, BF),
            V((krows, pcols, width), BF),
            V((krows, pcols, width), BF),
            V(tokens.shape, BF),
            V((krows, pcols, 128), BF),
            V((krows, pcols, 128), BF),
            V((rows, cols, 128), BF),
            V(tokens.shape, BF),
            V((steps + 1, npq, width + 256), F32),
            V((steps, npq, width + 256), F32),
            pltpu.SemaphoreType.DMA((8,)),
            pltpu.SemaphoreType.DMA((2,)),
            pltpu.SemaphoreType.DMA((2,)),
            pltpu.SemaphoreType.DMA((steps,)),
            pltpu.SemaphoreType.DMA((steps,)),
        ],
        compiler_params=pltpu.CompilerParams(
            collective_id=0, has_side_effects=True, vmem_limit_bytes=63 * 1024 * 1024),
    )(tokens, wq, wk, wv, wo, pick, table, pool_queries, norm_gain, head_scale)


def solution(mesh):
    placed = (P(("slide", "row"), None, None), P(), P(), P(), P(), P(), P(), P())
    return jax.shard_map(
        functools.partial(per_device, mesh.shape["row"]),
        mesh=mesh,
        in_specs=placed,
        out_specs=(P(("slide", "row"), None, None), P("slide", None)),
        check_vma=False,
    )
```

```python
import functools
import math

import jax
import jax.numpy as jnp
import numpy as np
from jax import lax
from jax.experimental import pallas as pl
from jax.experimental.pallas import tpu as pltpu
from jax.sharding import PartitionSpec as P

RAD = 4
EPS = 1e-06
PAD = 8
BLOCK = 32
WIN = BLOCK + 2 * PAD
RING = 48
LOG2E = math.log2(math.e)
FAR = -(2.0**30)
MESH = pl.DeviceIdType.MESH
BF = jnp.bfloat16
F32 = jnp.float32
NT = (((1,), (1,)), ((), ()))


def tables(heads, width, rows, cols):
    hw = width // heads
    t6, t3 = 6 * heads, 3 * heads
    row0, col0 = t6, t6 + rows
    pool_lane = col0 + RING
    assert pool_lane < 128
    lane = np.arange(128)
    head_of = np.arange(width) // hw
    ek = ((lane[None] // 6 == head_of[:, None]) & (lane[None] < t6)).astype(np.float32)
    ev = ((lane[None] // 3 == head_of[:, None]) & (lane[None] < t3)).astype(np.float32)
    sel = np.full((8, 128), 3.0, np.float32)
    sel[0, :t6] = np.tile([0, 1, 0, 1, 2, 0], heads)
    sel[1, :t6] = np.tile([0, 0, 1, 1, 0, 2], heads)
    sel[2, :t3] = np.tile([0, 1, 2], heads)
    pc = np.arange(cols + 2 * PAD) - PAD
    inside = (pc >= 0) & (pc < cols)
    kcol = np.zeros((cols + 2 * PAD, 128), np.float32)
    m = np.arange(RING)
    near = ((pc[:, None] - m[None] + RAD) % RING <= 2 * RAD) & inside[:, None]
    kcol[:, col0 : col0 + RING] = np.where(near, 0.0, FAR)
    kcol[:, pool_lane] = np.where(inside, 0.0, FAR)
    qcol = np.zeros((cols, 128), np.float32)
    qcol[np.arange(cols), col0 + np.arange(cols) % RING] = 1.0
    return (
        jnp.asarray(np.stack([ek, ev]), BF), jnp.asarray(np.concatenate([sel, kcol, qcol])),
        row0, pool_lane,
    )


def kernel(
    n, heads, row0, pool_lane,
    tok_hbm, wq_hbm, wk_hbm, wv_hbm, wo_hbm, pick_hbm, table_hbm, pq_hbm, gain_ref, scale_ref,
    mixed_ref, pooled_ref,
    tok, wq, wk, wv, wo, picks, table, pq_ref, halo, nrm, nrmq, kk, vv, qq, kaug, vaug, qaug, att, st, rc,
    load_sem, tok_send, tok_recv, st_send, st_recv,
):
    rows, cols, width = tok.shape
    pcols = cols + 2 * PAD
    steps = n.bit_length() - 1
    pairs = width // 128
    hw = width // heads
    blocks = cols // BLOCK
    krows = rows + 2 * RAD
    npq = pq_ref.shape[0]
    ek_ref, ev_ref = picks.at[0], picks.at[1]
    sel_ref = table.at[pl.ds(0, 8)]
    kcol_ref = table.at[pl.ds(8, pcols)]
    qcol_ref = table.at[pl.ds(8 + pcols, cols)]
    nt = 256 if width % 256 == 0 else 128
    me = lax.axis_index("row")

    loads = [
        pltpu.make_async_copy(src, dst, load_sem.at[i])
        for i, (src, dst) in enumerate(
            [(tok_hbm, tok), (wk_hbm, wk), (wv_hbm, wv), (pick_hbm, picks), (table_hbm, table), (pq_hbm, pq_ref), (wq_hbm, wq), (wo_hbm, wo)]
        )
    ]
    for load in loads:
        load.start()

    partners = [me + (1 - 2 * ((me // (1 << k)) % 2)) * (1 << k) for k in range(steps)]
    barrier = pltpu.get_barrier_semaphore()

    def signal(to):
        pl.semaphore_signal(barrier, inc=1, device_id={"row": to}, device_id_type=MESH)

    beside = lax.rem(me + n - 1 + 2 * (me % 2), n)
    for other in partners + [beside]:
        signal(other)
    pl.semaphore_wait(barrier, steps + 1)

    to_left = pltpu.make_async_remote_copy(
        tok_hbm.at[pl.ds(0, RAD)], halo.at[1], tok_send.at[0], tok_recv.at[1],
        device_id={"row": jnp.maximum(me - 1, 0)}, device_id_type=MESH)
    to_right = pltpu.make_async_remote_copy(
        tok_hbm.at[pl.ds(rows - RAD, RAD)], halo.at[0], tok_send.at[1], tok_recv.at[0],
        device_id={"row": jnp.minimum(me + 1, n - 1)}, device_id_type=MESH)
    even = me % 2 == 0
    pl.when(jnp.logical_and(even, me > 0))(lambda: to_left.start())
    pl.when(me < n - 1)(lambda: to_right.start())
    pl.when(jnp.logical_not(even))(lambda: to_left.start())

    lane = lax.broadcasted_iota(jnp.int32, (1, 128), 1)
    gain = gain_ref[...].reshape(1, width)

    def normalized(x):
        x = x.astype(F32)
        return x * lax.rsqrt(jnp.mean(x * x, axis=-1, keepdims=True) + EPS) * gain

    def padded(y):
        zero = jnp.zeros((PAD, y.shape[1]), F32)
        return jnp.concatenate([zero, y, zero], axis=0).astype(BF)

    def split(t, kind):
        hi = t.astype(BF).astype(F32)
        mid = (t - hi).astype(BF).astype(F32)
        low = t - hi - mid
        kind = sel_ref[kind : kind + 1, :]
        return jnp.where(kind == 0, hi, jnp.where(kind == 1, mid, jnp.where(kind == 2, low, 0.0)))

    def times(u, pick):
        u = u.astype(F32)
        sq = u * u
        hi = sq.astype(BF)
        low = (sq - hi.astype(F32)).astype(BF)
        total = jnp.dot(hi, pick, preferred_element_type=F32)
        total = total + jnp.dot(low, pick, preferred_element_type=F32)
        return jnp.sqrt(1.0 + total)

    def keys_values(first, count):
        flat = nrm[pl.ds(first, count)].reshape(count * pcols, width)

        def tile(j, _):
            part = pl.ds(pl.multiple_of(j * nt, nt), nt)
            k = jnp.dot(flat, wk[:, part], preferred_element_type=F32).astype(BF)
            kk[pl.ds(first, count), :, part] = k.reshape(count, pcols, nt)
            v = jnp.dot(flat, wv[:, part], preferred_element_type=F32).astype(BF)
            vv[pl.ds(first, count), :, part] = v.reshape(count, pcols, nt)
            return 0

        lax.fori_loop(0, width // nt, tile, 0)

        def aug(i, _):
            slot = first + i
            inside = jnp.logical_and(
                jnp.logical_or(slot >= RAD, me > 0), jnp.logical_or(slot < RAD + rows, me < n - 1))
            qrow = lane - row0
            seen = (qrow <= slot) & (qrow >= slot - 2 * RAD) & inside
            row_mask = jnp.where((qrow >= 0) & (qrow < rows) & ~seen, FAR, 0.0)
            kaug[slot] = (split(times(kk[slot], ek_ref[...]), 0) + row_mask + kcol_ref[...]).astype(BF)
            vaug[slot] = split(times(vv[slot], ev_ref[...]), 2).astype(BF)
            return 0

        lax.fori_loop(0, count, aug, 0)

    loads[0].wait()

    def own_norm(r, _):
        y = normalized(tok[r])
        nrmq[r] = y.astype(BF)
        nrm[RAD + r] = padded(y)
        return 0

    lax.fori_loop(0, rows, own_norm, 0)
    for load in loads[1:6]:
        load.wait()
    keys_values(RAD, rows)

    def head_pair(q, aug, p):
        zero = jnp.zeros((), BF)
        low = lane < hw
        out = []
        for i in range(2):
            h = 2 * p + i
            mine = low if i == 0 else ~low
            keep = ((lane >= 6 * h) & (lane < 6 * h + 6)) | (lane >= row0)
            out.append(jnp.concatenate(
                [jnp.where(mine, q, zero), jnp.where(keep, aug, zero)], axis=1))
        return jnp.concatenate(out, axis=0)

    pq_aug = (jnp.where(lane == pool_lane, 1.0, 0.0) - split(times(pq_ref[...], ek_ref[...]), 1)).astype(BF)

    own = pl.ds(RAD, rows)
    peaks = jnp.full((npq, 128), 0.0, F32)
    tsum = jnp.full((npq, 128), 1.0, F32)
    for p in range(pairs):
        part = pl.ds(128 * p, 128)
        keys = jnp.concatenate(
            [kk[own, :, part].reshape(rows * pcols, 128), kaug[own].reshape(rows * pcols, 128)], axis=1)
        vals = jnp.concatenate(
            [vv[own, :, part].reshape(rows * pcols, 128), vaug[own].reshape(rows * pcols, 128)], axis=1)
        d = lax.dot_general(head_pair(pq_ref[:, part], pq_aug, p), keys, NT, preferred_element_type=F32)
        top = jnp.max(d, axis=-1, keepdims=True)
        scaled = []
        for i in range(2):
            c = (2.0 * LOG2E) * scale_ref[2 * p + i]
            mine = slice(i * npq, (i + 1) * npq)
            scaled.append((d[mine] - top[mine]) * c)
            peaks = jnp.where(lane == 2 * p + i, top[mine] * c, peaks)
        f = jnp.exp2(jnp.concatenate(scaled, axis=0))
        hi = f.astype(BF)
        rest = f - hi.astype(F32)
        mid = rest.astype(BF)
        low = (rest - mid.astype(F32)).astype(BF)
        m = jnp.dot(jnp.concatenate([hi, mid, low], axis=0), vals, preferred_element_type=F32)
        m = m[: 2 * npq] + m[2 * npq : 4 * npq] + m[4 * npq :]
        st[0, :, part] = jnp.where(lane < hw, m[:npq, :128], m[npq:, :128])
        for i in range(2):
            h = 2 * p + i
            tv = jnp.where((lane >= 3 * h) & (lane < 3 * h + 3), m[i * npq : (i + 1) * npq, 128:], 0.0)
            tsum = jnp.where(lane == h, jnp.sum(tv, axis=-1, keepdims=True), tsum)
    st[0, :, width : width + 128] = peaks
    st[0, :, width + 128 : width + 256] = tsum

    swaps = [
        pltpu.make_async_remote_copy(
            st.at[k], rc.at[k], st_send.at[k], st_recv.at[k],
            device_id={"row": partners[k]}, device_id_type=MESH)
        for k in range(steps)
    ]
    swaps[0].start()

    def spread_heads(x, p):
        return jnp.where(lane < hw, x[:, 2 * p : 2 * p + 1], x[:, 2 * p + 1 : 2 * p + 2])

    def merge(k):
        swaps[k].wait()
        peak_mine, peak_other = st[k, :, width : width + 128], rc[k, :, width : width + 128]
        peak = jnp.maximum(peak_mine, peak_other)
        f_mine, f_other = jnp.exp2(peak_mine - peak), jnp.exp2(peak_other - peak)
        st[k + 1, :, width : width + 128] = peak
        tpart = pl.ds(width + 128, 128)
        st[k + 1, :, tpart] = st[k, :, tpart] * f_mine + rc[k, :, tpart] * f_other
        for p in range(pairs):
            part = pl.ds(128 * p, 128)
            a = st[k, :, part] * spread_heads(f_mine, p)
            b = rc[k, :, part] * spread_heads(f_other, p)
            st[k + 1, :, part] = a + b
        if k + 1 < steps:
            swaps[k + 1].start()

    loads[6].wait()

    def query_tile(j, _):
        part = pl.ds(pl.multiple_of(j * nt, nt), nt)
        q = jnp.dot(nrmq[...].reshape(rows * cols, width), wq[:, part], preferred_element_type=F32)
        qq[:, :, part] = q.astype(BF).reshape(rows, cols, nt)
        return 0

    lax.fori_loop(0, width // nt, query_tile, 0)

    def query_aug(r, _):
        onehot = jnp.where(lane == row0 + r, 1.0, 0.0)
        qaug[r] = (qcol_ref[...] + onehot - split(times(qq[r], ek_ref[...]), 1)).astype(BF)
        return 0

    lax.fori_loop(0, rows, query_aug, 0)

    merge(0)

    def arrived(i):
        pltpu.make_async_remote_copy(
            tok_hbm.at[pl.ds(0, RAD)], halo.at[i], tok_send.at[i], tok_recv.at[i],
            device_id={"row": beside}, device_id_type=MESH).wait_recv()

    def side_rows(i, first):
        def norm(r, _):
            nrm[first + r] = padded(normalized(halo[i, r]))
            return 0

        lax.fori_loop(0, RAD, norm, 0)
        keys_values(first, RAD)

    near, far = 1 - me % 2, me % 2
    inner = jnp.logical_and(me > 0, me < n - 1)
    arrived(near)
    side_rows(near, near * (RAD + rows))

    @pl.when(inner)
    def _():
        arrived(far)

    @pl.when(jnp.logical_not(inner))
    def _():
        halo[far] = jnp.zeros(halo.shape[1:], BF)

    side_rows(far, far * (RAD + rows))

    def attend(p, _):
        part = pl.ds(pl.multiple_of(128 * p, 128), 128)
        c0 = (2.0 * LOG2E) * scale_ref[2 * p]
        c1 = (2.0 * LOG2E) * scale_ref[2 * p + 1]
        for b in range(blocks):
            qs, ks = pl.ds(b * BLOCK, BLOCK), pl.ds(b * BLOCK, WIN)
            nq, nk = rows * BLOCK, krows * WIN
            q = head_pair(qq[:, qs, part].reshape(nq, 128), qaug[:, qs, :].reshape(nq, 128), p)
            keys = jnp.concatenate(
                [kk[:, ks, part].reshape(nk, 128), kaug[:, ks, :].reshape(nk, 128)], axis=1)
            vals = jnp.concatenate(
                [vv[:, ks, part].reshape(nk, 128), vaug[:, ks, :].reshape(nk, 128)], axis=1)
            d = lax.dot_general(q, keys, NT, preferred_element_type=F32)
            d = d - jnp.max(d, axis=-1, keepdims=True)
            e = jnp.concatenate([jnp.exp2(d[:nq] * c0), jnp.exp2(d[nq:] * c1)], axis=0).astype(BF)
            m = jnp.dot(e, vals, preferred_element_type=F32)
            out = []
            for i in range(2):
                h = 2 * p + i
                sp, tv = m[i * nq : (i + 1) * nq, :128], m[i * nq : (i + 1) * nq, 128:]
                mine = (lane < hw) if i == 0 else (lane >= hw)
                mt = jnp.sum(jnp.where((lane >= 3 * h) & (lane < 3 * h + 3), tv, 0.0), axis=-1, keepdims=True)
                ss = jnp.sum(jnp.where(mine, sp * sp, 0.0), axis=-1, keepdims=True)
                out.append(sp * lax.rsqrt(mt * mt - ss))
            att[:, qs, part] = jnp.where(lane < hw, out[0], out[1]).astype(BF).reshape(rows, BLOCK, 128)
        for k in range(1, steps):
            pl.when(p == (k - 1) * pairs // max(steps - 1, 1))(functools.partial(merge, k))
        return 0

    lax.fori_loop(0, pairs, attend, 0)

    last = st.at[steps]
    mt = last[:, width + 128 : width + 256]
    for p in range(pairs):
        part = pl.ds(128 * p, 128)
        sp = last[:, part]
        sq = sp * sp
        ss = jnp.where(
            lane < hw,
            jnp.sum(jnp.where(lane < hw, sq, 0.0), axis=-1, keepdims=True),
            jnp.sum(jnp.where(lane < hw, 0.0, sq), axis=-1, keepdims=True))
        t = spread_heads(mt, p)
        pooled_ref[:, part] = sp / jnp.sqrt(t * t - ss)

    loads[7].wait()

    def out_tile(j, _):
        part = pl.ds(pl.multiple_of(j * nt, nt), nt)
        y = jnp.dot(att[...].reshape(rows * cols, width), wo[:, part], preferred_element_type=F32)
        y = y + tok[:, :, part].reshape(rows * cols, nt).astype(F32)
        mixed_ref[:, :, part] = y.astype(BF).reshape(rows, cols, nt)
        return 0

    lax.fori_loop(0, width // nt, out_tile, 0)
    pl.when(me > 0)(lambda: to_left.wait_send())
    pl.when(me < n - 1)(lambda: to_right.wait_send())


def per_device(n, tokens, norm_gain, wq, wk, wv, wo, head_scale, pool_queries):
    rows, cols, width = tokens.shape
    heads = head_scale.shape[0]
    npq = pool_queries.shape[0]
    steps = n.bit_length() - 1
    assert n == 1 << steps and rows >= RAD and cols % BLOCK == 0 and 2 * width == 128 * heads
    pick, table, row0, pool_lane = tables(heads, width, rows, cols)
    krows, pcols = rows + 2 * RAD, cols + 2 * PAD
    vm = pl.BlockSpec(memory_space=pltpu.VMEM)
    hbm = pl.BlockSpec(memory_space=pltpu.HBM)
    V = pltpu.VMEM
    wshape = V((width, width), BF)
    return pl.pallas_call(
        functools.partial(kernel, n, heads, row0, pool_lane),
        out_shape=(
            jax.ShapeDtypeStruct(tokens.shape, BF),
            jax.ShapeDtypeStruct((npq, width), F32),
        ),
        in_specs=[hbm] * 8 + [vm, pl.BlockSpec(memory_space=pltpu.SMEM)],
        out_specs=(vm, vm),
        scratch_shapes=[
            V(tokens.shape, BF), wshape, wshape, wshape, wshape,
            V(pick.shape, BF), V(table.shape, F32), V(pool_queries.shape, BF),
            V((2, RAD, cols, width), BF),
            V((krows, pcols, width), BF),
            V(tokens.shape, BF),
            V((krows, pcols, width), BF),
            V((krows, pcols, width), BF),
            V(tokens.shape, BF),
            V((krows, pcols, 128), BF),
            V((krows, pcols, 128), BF),
            V((rows, cols, 128), BF),
            V(tokens.shape, BF),
            V((steps + 1, npq, width + 256), F32),
            V((steps, npq, width + 256), F32),
            pltpu.SemaphoreType.DMA((8,)),
            pltpu.SemaphoreType.DMA((2,)),
            pltpu.SemaphoreType.DMA((2,)),
            pltpu.SemaphoreType.DMA((steps,)),
            pltpu.SemaphoreType.DMA((steps,)),
        ],
        compiler_params=pltpu.CompilerParams(
            collective_id=0, has_side_effects=True, vmem_limit_bytes=63 * 1024 * 1024),
    )(tokens, wq, wk, wv, wo, pick, table, pool_queries, norm_gain, head_scale)


def solution(mesh):
    placed = (P(("slide", "row"), None, None), P(), P(), P(), P(), P(), P(), P())
    return jax.shard_map(
        functools.partial(per_device, mesh.shape["row"]),
        mesh=mesh,
        in_specs=placed,
        out_specs=(P(("slide", "row"), None, None), P("slide", None)),
        check_vma=False,
    )
```
